128 devices in a mesh: sky: 8 (over x, core), det: 16 (over z, y).
Axes of the slice: x: 4, y: 4, z: 4, core: 2. Of those that a mesh axis runs over, the one named last changes fastest.
Arguments:
- templates: bfloat16 [256, 512, 512], P(('sky', 'det')), may hold values from -6 to 6
- science: bfloat16 [256, 512, 512], P(('sky', 'det')), may hold values from -6 to 6
- intersection: int32 [256, 4], P(('sky', 'det')), may hold values from 0 to 63, as said below
- row_warp: int32 [256, 4], P(('sky', 'det')), may hold values from 0 to 7
- col_warp: int32 [256, 4], P(('sky', 'det')), may hold values from 0 to 7
- warps: bfloat16 [8, 512, 512], replicated, may hold values from -0.25 to 0.25
- taps: float32 [16, 21], replicated, may hold values from -1.25 to 1.25
- basis_row: int32 [256, 5], P(('sky', 'det')), may hold values from 0 to 15
- basis_col: int32 [256, 5], P(('sky', 'det')), may hold values from 0 to 15
- coef: float32 [256, 5, 3], P(('sky', 'det')), may hold values from -4 to 4
- home: int32 [256], P(('sky', 'det')), may hold values from 0 to 31, as said below
Outputs:
- returned: bfloat16 [4096, 512, 512], P(('sky', 'det'))
The draws below stay inside these ranges and needn't reach their ends.
Inputs may be any that keep to these rules, and one draw needn't show every extreme that they name: `intersection`: among the 8 entries q of one device's detector tiles, at most 2 share a value of (q // 2) % 16, and 2 is reached by some value in every such group. `home`: the 2 values of one device's detector tiles are distinct and share one value of home // 2, so both difference tiles of a device go to the same det index.
All inputs are finite; a program needn't handle non-finite values.
Results may differ from the reference program's by a relative error of at most 0.019.
Values may be sent and summed in bfloat16 or wider, within the bound.
No kernel may reach another device: no remote copies, remote signals or barrier semaphores. Data moves between devices by JAX's collectives and lax.ppermute only.
A program may use at most 192 MiB of HBM per device.

```python
import jax
import jax.numpy as jnp
from jax import lax

SIDE = 512
TGT_DEV = 2
INTERSECTIONS = 4
BANK = 8
FILTERS = 16
BASES = 5
TAPS = 21
TPL_DEV = 2
CAP = 2
CAP_BACK = 2
TARGETS = 256
TEMPLATES = 256
RETURNED = 4096
N_SKY = 8
N_DET = 16


def pick_slots(key, blocks, rows, owners, limit):

    def one_block(block_key):
        first, second, third = jax.random.split(block_key, 3)
        filled = jax.random.randint(first, (), 0, owners)
        shuffled = jax.random.permutation(second, owners * limit)
        later = jnp.where(shuffled // limit == filled, 0, 1)
        order = jnp.argsort(later * (owners * limit) + jnp.arange(owners * limit), stable=True)
        chosen = shuffled[order][:rows]
        return chosen[jax.random.permutation(third, rows)]
    return jax.vmap(one_block)(jax.random.split(key, blocks))


def draw_intersection(key, part):
    key = jax.random.fold_in(key, 11)
    slots = pick_slots(key, N_SKY * N_DET, TGT_DEV * INTERSECTIONS, N_DET, CAP)
    owner = slots // CAP
    local = jax.random.randint(jax.random.fold_in(key, 5), slots.shape, 0, 2 * TPL_DEV)
    value = local // TPL_DEV * (N_DET * TPL_DEV) + owner * TPL_DEV + local % TPL_DEV
    return value.reshape(TARGETS, INTERSECTIONS).astype(jnp.int32)


def draw_home(key, part):
    key = jax.random.fold_in(key, 23)
    slots = pick_slots(key, N_SKY * N_DET, TGT_DEV, N_DET, CAP_BACK)
    return slots.reshape(TARGETS).astype(jnp.int32)


def with_ends(array, key, low, top_value):
    longest = array.shape.index(max(array.shape))
    spots = []
    for shift in (0, 1):
        where = [jax.random.randint(jax.random.fold_in(key, axis), (), 0, length) for axis, length in enumerate(array.shape)]
        where[longest] = (where[longest] + shift) % array.shape[longest]
        spots.append(tuple(where))
    return array.at[spots[0]].set(low).at[spots[1]].set(top_value)


def shard_levels(rng, dims, shards, least, top_value):
    factor_of, own = 1.0, jax.random.fold_in(rng, 6)
    for axis_at, shards_of in shards:
        heights = jnp.exp(jax.random.uniform(jax.random.fold_in(own, axis_at), (shards_of,), jnp.float32, least / len(shards), top_value / len(shards)))
        factor_of = factor_of * jnp.repeat(heights, dims[axis_at] // shards_of).reshape([-1 if axis == axis_at else 1 for axis in range(len(dims))])
    return factor_of


def scatter_about(stream_key, shape, deviation, most, cuts=(), held_as=jnp.bfloat16):
    array = deviation * jax.random.normal(stream_key, shape, jnp.float32)
    if cuts:
        array = array * shard_levels(stream_key, shape, cuts, -0.22, 0.18)
    return jnp.clip(array, -most, most).astype(held_as)


def setup_inputs(seed: int = 0) -> dict:
    splits = jax.random.split(jax.random.key(seed), 12)
    return {
        "templates": scatter_about(splits[0], (TEMPLATES, SIDE, SIDE), 1.0, 6.0, ((0, 128),)),
        "science": scatter_about(splits[1], (TARGETS, SIDE, SIDE), 1.0, 6.0, ((0, 128),)),
        "intersection": draw_intersection(jax.random.fold_in(splits[11], 71), 0),
        "row_warp": with_ends(jax.random.randint(splits[3], (TARGETS, INTERSECTIONS), 0, BANK), jax.random.fold_in(splits[3], 1), 0, BANK - 1).astype(jnp.int32),
        "col_warp": with_ends(jax.random.randint(splits[4], (TARGETS, INTERSECTIONS), 0, BANK), jax.random.fold_in(splits[4], 1), 0, BANK - 1).astype(jnp.int32),
        "warps": scatter_about(splits[5], (BANK, SIDE, SIDE), SIDE ** -0.5, 0.25),
        "taps": scatter_about(splits[6], (FILTERS, TAPS), TAPS ** -0.5, 1.25, (), jnp.float32),
        "basis_row": with_ends(jax.random.randint(splits[7], (TARGETS, BASES), 0, FILTERS), jax.random.fold_in(splits[7], 1), 0, FILTERS - 1).astype(jnp.int32),
        "basis_col": with_ends(jax.random.randint(splits[8], (TARGETS, BASES), 0, FILTERS), jax.random.fold_in(splits[8], 1), 0, FILTERS - 1).astype(jnp.int32),
        "coef": scatter_about(splits[9], (TARGETS, BASES, 3), 0.7, 4.0, ((0, 128),), jnp.float32),
        "home": draw_home(jax.random.fold_in(splits[11], 71), 0),
    }


def make_bands(taps):
    width = taps.shape[1]
    offsets = jnp.arange(SIDE)[None, :] - jnp.arange(SIDE)[:, None] + width // 2
    selector = (jnp.arange(width)[:, None, None] == offsets[None]).astype(jnp.float32)
    bands = jnp.einsum("tij,ft->fij", selector, taps.astype(jnp.float32), precision=lax.Precision.HIGHEST)
    return bands.astype(jnp.bfloat16)


def reference(templates, science, intersection, row_warp, col_warp, warps, taps, basis_row, basis_col, coef, home):
    bands = make_bands(taps)
    target = jnp.arange(TARGETS, dtype=jnp.int32)
    patch = target // (N_DET * TGT_DEV)
    detidx = (target // TGT_DEV) % N_DET
    which = intersection // (N_DET * TPL_DEV)
    source = ((patch[:, None] + which) % N_SKY) * (N_DET * TPL_DEV) + intersection % (N_DET * TPL_DEV)
    source = source.astype(jnp.int32)
    coord = (2.0 * jnp.arange(SIDE, dtype=jnp.float32) + 1.0) / SIDE - 1.0

    def one_tile(items):
        src, rwi, cwi, bri, bci, cof, sci = items
        tiles = templates[src].astype(jnp.float32)
        left = warps[rwi].astype(jnp.float32)
        right = warps[cwi].astype(jnp.float32)
        inner = jnp.einsum("nij,njk->nik", left, tiles).astype(jnp.bfloat16)
        piece = jnp.einsum("nik,nlk->nil", inner.astype(jnp.float32), right).astype(jnp.bfloat16)
        warped = jnp.sum(piece.astype(jnp.float32), axis=0).astype(jnp.bfloat16)
        rowband = bands[bri].astype(jnp.float32)
        colband = bands[bci].astype(jnp.float32)
        half = jnp.einsum("bij,jk->bik", rowband, warped.astype(jnp.float32)).astype(jnp.bfloat16)
        conv = jnp.einsum("bik,blk->bil", half.astype(jnp.float32), colband)
        field = cof[:, 0, None, None] + cof[:, 1, None, None] * coord[None, :, None] + cof[:, 2, None, None] * coord[None, None, :]
        model = jnp.sum(field * conv, axis=0)
        return (sci.astype(jnp.float32) - model).astype(jnp.bfloat16)

    diffs = lax.map(one_tile, (source, row_warp, col_warp, basis_row, basis_col, coef, science))
    rows = patch * (N_DET * N_DET * CAP_BACK) + (home // CAP_BACK) * (N_DET * CAP_BACK) + detidx * CAP_BACK + home % CAP_BACK
    rows = rows.astype(jnp.int32)
    returned = jnp.zeros((RETURNED, SIDE, SIDE), jnp.bfloat16).at[rows].set(diffs)
    return returned
```

```python
import functools

import jax
import jax.numpy as jnp
from jax import lax
from jax.experimental import pallas as pl
from jax.experimental.pallas import tpu as pltpu
from jax.sharding import PartitionSpec as P

SIDE = 512
RING = 4
TILES = 2
PER_TILE = 4
BASES = 5
ROUND = (0, 1, 3, 2)
VMEM_LIMIT = 56 * 1024 * 1024


def place(z, y):
    return (z % RING) * RING + y % RING


def hop(block, dz, dy):
    route = [
        (place(z, y), place(z + dz, y + dy)) for z in range(RING) for y in range(RING)
    ]
    return lax.ppermute(block, "det", route)


def along(block, axis, step):
    return hop(block, step, 0) if axis == "z" else hop(block, 0, step)


def next_patch(block):
    count = lax.axis_size("sky")
    return lax.ppermute(block, "sky", [((i + 1) % count, i) for i in range(count)])


def spread_small(block, axis):
    return jnp.stack([block] + [along(block, axis, -k) for k in range(1, RING)])


def make_bands(taps):
    width = taps.shape[1]
    offsets = jnp.arange(SIDE)[None, :] - jnp.arange(SIDE)[:, None] + width // 2
    selector = (jnp.arange(width)[:, None, None] == offsets[None]).astype(jnp.float32)
    bands = jnp.einsum("tij,ft->fij", selector, taps, precision=lax.Precision.HIGHEST)
    return bands.astype(jnp.bfloat16)


def warp_kernel(steps, where, meta, *refs):
    cands, (warps, out), scratch = refs[:10], refs[10:12], refs[12:]
    picks, tile, left, right, acc, sems = scratch
    z, y = where[0], where[1]
    count = jnp.int32(0)
    for n, step in enumerate(steps):
        for t in range(TILES):
            for k in range(PER_TILE):
                q = meta[step, 0, t * PER_TILE + k]
                owner = (q // TILES) % (RING * RING)
                picks[0, count] = (
                    q // (TILES * RING * RING) * (RING * TILES)
                    + ((owner // RING - z + RING) % RING) * TILES
                    + q % TILES
                )
                picks[1, count] = meta[step, 1, t * PER_TILE + k]
                picks[2, count] = meta[step, 2, t * PER_TILE + k]
                picks[3, count] = n * TILES + t
                count = count + (owner % RING == y).astype(jnp.int32)

    def tile_copy(slot, source):
        return pltpu.make_async_copy(source, tile.at[slot], sems.at[0, slot])

    def bank_copies(slot, row, col):
        return (
            pltpu.make_async_copy(warps.at[row], left.at[slot], sems.at[1, slot]),
            pltpu.make_async_copy(warps.at[col], right.at[slot], sems.at[2, slot]),
        )

    def start(i, slot):
        source = picks[0, i]
        for copy in bank_copies(slot, picks[1, i], picks[2, i]):
            copy.start()
        for which in range(2):
            for dz in range(RING):
                for local in range(TILES):

                    @pl.when(source == (which * RING + dz) * TILES + local)
                    def _():
                        if dz == 2:
                            ref = cands[which * 5 + 3 + local].at[0]
                        else:
                            ref = cands[which * 5 + {0: 0, 3: 1, 1: 2}[dz]].at[local]
                        tile_copy(slot, ref).start()

    @pl.when(count > 0)
    def _():
        start(0, 0)

    acc[...] = jnp.zeros_like(acc)

    def body(i, carry):
        slot = lax.rem(i, 2)
        tile_copy(slot, cands[0].at[0]).wait()
        for copy in bank_copies(slot, 0, 0):
            copy.wait()

        @pl.when(i + 1 < count)
        def _():
            start(i + 1, 1 - slot)

        inner = jnp.dot(left[slot], tile[slot], preferred_element_type=jnp.float32)
        piece = lax.dot_general(
            inner.astype(jnp.bfloat16),
            right[slot],
            (((1,), (1,)), ((), ())),
            preferred_element_type=jnp.float32,
        )
        target = picks[3, i]
        acc[target] = acc[target] + piece
        return carry

    lax.fori_loop(0, count, body, 0)
    out[...] = acc[...].astype(jnp.bfloat16)


def warp_partials(steps, where, meta, cands, warps):
    rows = len(steps) * TILES
    anywhere = pl.BlockSpec(memory_space=pl.ANY)
    scalars = pl.BlockSpec(memory_space=pltpu.SMEM)
    return pl.pallas_call(
        functools.partial(warp_kernel, steps),
        out_shape=jax.ShapeDtypeStruct((rows, SIDE, SIDE), jnp.bfloat16),
        in_specs=[scalars, scalars] + [anywhere] * 11,
        out_specs=pl.BlockSpec(memory_space=pltpu.VMEM),
        scratch_shapes=[
            pltpu.SMEM((4, rows * PER_TILE + 1), jnp.int32),
            pltpu.VMEM((2, SIDE, SIDE), jnp.bfloat16),
            pltpu.VMEM((2, SIDE, SIDE), jnp.bfloat16),
            pltpu.VMEM((2, SIDE, SIDE), jnp.bfloat16),
            pltpu.VMEM((rows, SIDE, SIDE), jnp.float32),
            pltpu.SemaphoreType.DMA((3, 2)),
        ],
        compiler_params=pltpu.CompilerParams(vmem_limit_bytes=VMEM_LIMIT),
        cost_estimate=pl.CostEstimate(
            flops=rows * 4 * SIDE**3, bytes_accessed=rows * 4 * SIDE**2 * 2, transcendentals=0
        ),
    )(where, meta, *cands, warps)


def match_kernel(picks, coef, row, col, first, second, third, science, out, warped, model):
    b = pl.program_id(0)

    @pl.when(b == 0)
    def _():
        total = first[...].astype(jnp.float32) + second[...].astype(jnp.float32)
        warped[...] = (total + third[...].astype(jnp.float32)).astype(jnp.bfloat16)
        model[...] = jnp.zeros_like(model)

    half = jnp.dot(row[...], warped[...], preferred_element_type=jnp.float32)
    conv = lax.dot_general(
        half.astype(jnp.bfloat16),
        col[...],
        (((1,), (1,)), ((), ())),
        preferred_element_type=jnp.float32,
    )
    shape = (SIDE, SIDE)
    ui = (2.0 * lax.broadcasted_iota(jnp.int32, shape, 0).astype(jnp.float32) + 1.0) / SIDE - 1.0
    uj = (2.0 * lax.broadcasted_iota(jnp.int32, shape, 1).astype(jnp.float32) + 1.0) / SIDE - 1.0
    model[...] += (coef[b, 0] + coef[b, 1] * ui + coef[b, 2] * uj) * conv

    @pl.when(b == pl.num_programs(0) - 1)
    def _():
        out[...] = (science[...].astype(jnp.float32) - model[...]).astype(jnp.bfloat16)


def match(rows, cols, coef, bands, parts, science):
    whole = pl.BlockSpec((SIDE, SIDE), lambda b, picks: (0, 0))
    return pl.pallas_call(
        match_kernel,
        out_shape=jax.ShapeDtypeStruct((SIDE, SIDE), jnp.bfloat16),
        grid_spec=pltpu.PrefetchScalarGridSpec(
            num_scalar_prefetch=1,
            grid=(BASES,),
            in_specs=[
                pl.BlockSpec(memory_space=pltpu.SMEM),
                pl.BlockSpec((None, SIDE, SIDE), lambda b, picks: (picks[0, b], 0, 0)),
                pl.BlockSpec((None, SIDE, SIDE), lambda b, picks: (picks[1, b], 0, 0)),
                whole,
                whole,
                whole,
                whole,
            ],
            out_specs=whole,
            scratch_shapes=[
                pltpu.VMEM((SIDE, SIDE), jnp.bfloat16),
                pltpu.VMEM((SIDE, SIDE), jnp.float32),
            ],
        ),
        compiler_params=pltpu.CompilerParams(vmem_limit_bytes=VMEM_LIMIT),
        cost_estimate=pl.CostEstimate(
            flops=BASES * 4 * SIDE**3, bytes_accessed=BASES * 4 * SIDE**2 * 2, transcendentals=0
        ),
    )(jnp.stack([rows, cols]), coef, bands, bands, *parts, science)


def ring_gather(items, axis):
    other = {"z": 0, "y": 1}[axis]

    def moved(part, step, array, rows=None):
        away = list(part[1])
        away[other] -= step
        return (rows or part[0], tuple(away), array)

    found = list(items)
    if len(items) == 1:
        (part,) = items
        (low, high) = part[0]
        mid = (low + high) // 2
        ahead = moved(part, 1, along(part[2], axis, 1))
        back = moved(part, -1, along(part[2], axis, -1))
        found += [ahead, back]
        found.append(moved(ahead, 1, along(ahead[2][: mid - low], axis, 1), (low, mid)))
        found.append(moved(back, -1, along(back[2][mid - low :], axis, -1), (mid, high)))
        return found
    first = []
    for part in items:
        for step in (1, -1):
            first.append(moved(part, step, along(part[2], axis, step)))
    for n, step in enumerate((1, -1, 1, -1, -1)):
        part = first[2 * n + (0 if step == 1 else 1)]
        first.append(moved(part, step, along(part[2], axis, step)))
    return found + first


def return_kernel(plan, where, homes, *refs):
    arrays, out, sems = refs[: len(plan)], refs[-2], refs[-1]
    z, y = where[0], where[1]
    me = z * RING + y
    copies = []
    for n, (t, (low, high), (dz, dy)) in enumerate(plan):
        home = homes[dz % RING, dy % RING, t]
        source = ((z + dz + RING) % RING) * RING + (y + dy + RING) % RING
        slot = source * TILES + home % TILES
        copy = pltpu.make_async_copy(
            arrays[n], out.at[slot, pl.ds(low, high - low)], sems.at[n]
        )
        copies.append((home // TILES == me, copy))
    for live, copy in copies:
        pl.when(live)(copy.start)
    for live, copy in copies:
        pl.when(live)(copy.wait)


def give_back(where, homes, parts, blank):
    plan = [(t, rows, away) for t, found in enumerate(parts) for rows, away, _ in found]
    arrays = [array for found in parts for _, _, array in found]
    anywhere = pl.BlockSpec(memory_space=pl.ANY)
    scalars = pl.BlockSpec(memory_space=pltpu.SMEM)
    return pl.pallas_call(
        functools.partial(return_kernel, plan),
        out_shape=jax.ShapeDtypeStruct(blank.shape, blank.dtype),
        in_specs=[scalars, scalars] + [anywhere] * (len(plan) + 1),
        out_specs=anywhere,
        scratch_shapes=[pltpu.SemaphoreType.DMA((len(plan),))],
        input_output_aliases={len(plan) + 2: 0},
        compiler_params=pltpu.CompilerParams(vmem_limit_bytes=VMEM_LIMIT),
    )(where, homes, *arrays, blank)


def shards(
    templates,
    science,
    intersection,
    row_warp,
    col_warp,
    warps,
    taps,
    basis_row,
    basis_col,
    coef,
    home,
):
    me = lax.axis_index("det")
    where = jnp.stack([me // RING, me % RING]).astype(jnp.int32)

    with jax.named_scope("gather_templates"):
        before = along(templates, "z", 1)
        after = along(templates, "z", -1)
        far = (along(before[:1], "z", 1), along(after[1:], "z", -1))
        own = (templates, before, after) + far
        cands = own + tuple(next_patch(block) for block in own)

    with jax.named_scope("spread_tables"):
        table = jnp.concatenate(
            [
                intersection.reshape(-1),
                row_warp.reshape(-1),
                col_warp.reshape(-1),
                jnp.pad(home, (0, TILES * PER_TILE - TILES)),
            ]
        ).reshape(4, TILES * PER_TILE)
        meta = spread_small(table, "y")
        homes = spread_small(meta[:, 3, :TILES], "z")

    bands = make_bands(taps)
    blank = jnp.zeros((RING * RING * TILES, SIDE, SIDE), jnp.bfloat16)

    with jax.named_scope("warp"):
        opposite = warp_partials((2,), where, meta, cands, warps)
        nearer = warp_partials((0, 1, 3), where, meta, cands, warps)

    with jax.named_scope("sum_partials"):
        up = along(opposite[0], "y", 1)
        down = along(opposite[1], "y", -1)

        def plus(a, b):
            return (a.astype(jnp.float32) + b.astype(jnp.float32)).astype(jnp.bfloat16)

        parts = (
            (nearer[0], along(plus(nearer[2], up), "y", 1), along(nearer[4], "y", -1)),
            (nearer[1], along(nearer[3], "y", 1), along(plus(nearer[5], down), "y", -1)),
        )

    with jax.named_scope("match"):
        diffs = [
            match(basis_row[t], basis_col[t], coef[t], bands, parts[t], science[t])
            for t in range(TILES)
        ]

    with jax.named_scope("spread_differences"):
        whole = (0, SIDE)
        first = ring_gather(ring_gather([(whole, (0, 0), diffs[0])], "z"), "y")
        second = ring_gather(ring_gather([(whole, (0, 0), diffs[1])], "y"), "z")

    with jax.named_scope("give_back"):
        return give_back(where, homes, (first, second), blank)


def solution(mesh):
    placed = (
        P(("sky", "det"), None, None),
        P(("sky", "det"), None, None),
        P(("sky", "det"), None),
        P(("sky", "det"), None),
        P(("sky", "det"), None),
        P(),
        P(),
        P(("sky", "det"), None),
        P(("sky", "det"), None),
        P(("sky", "det"), None, None),
        P(("sky", "det")),
    )
    return jax.shard_map(
        shards, mesh=mesh, in_specs=placed, out_specs=P(("sky", "det"), None, None), check_vma=False
    )
```

```python
import functools

import jax
import jax.numpy as jnp
from jax import lax
from jax.experimental import pallas as pl
from jax.experimental.pallas import tpu as pltpu
from jax.sharding import PartitionSpec as P

SIDE = 512
RING = 4
TILES = 2
PER_TILE = 4
BASES = 5
REACH = 10
CHUNKS = RING * RING
CHUNK = TILES * SIDE // CHUNKS
PER_CHUNK = CHUNKS // TILES
LEVELS = (3, 4, 5, 6, 8, 16)
DEEP = 4
MIB = 1024 * 1024


def place(z, y):
    return (z % RING) * RING + y % RING


def hop(block, dz, dy):
    route = [
        (place(z, y), place(z + dz, y + dy)) for z in range(RING) for y in range(RING)
    ]
    return lax.ppermute(block, "det", route)


def along(block, axis, step):
    return hop(block, step, 0) if axis == "z" else hop(block, 0, step)


def next_patch(block, first=0, every=1):
    count = lax.axis_size("sky")
    route = [((i + 1) % count, i) for i in range(first, count, every)]
    return lax.ppermute(block, "sky", route)


def along_odd(block, step):
    route = [
        (sky * CHUNKS + place(z, y), sky * CHUNKS + place(z + step, y))
        for sky in range(1, lax.axis_size("sky"), 2)
        for z in range(RING)
        for y in range(RING)
    ]
    return lax.ppermute(block, ("sky", "det"), route)


def all_rows(row, axis):
    copies = jnp.broadcast_to(row, (lax.axis_size(axis), row.shape[0]))
    return lax.all_to_all(copies, axis, split_axis=0, concat_axis=0, tiled=True)


def together(*arrays):
    return lax.optimization_barrier(arrays)


def bands_kernel(taps, out):
    shape = (SIDE, SIDE)
    rows = lax.broadcasted_iota(jnp.int32, shape, 0)
    cols = lax.broadcasted_iota(jnp.int32, shape, 1)
    rolled = pltpu.roll(jnp.broadcast_to(taps[0], shape), 0, 1, stride=1, stride_axis=0)
    out[...] = jnp.where(jnp.abs(cols - rows) <= REACH, rolled, 0.0).astype(jnp.bfloat16)


def make_bands(taps):
    filters, width = taps.shape
    assert width == 2 * REACH + 1
    first_rows = jnp.roll(jnp.pad(taps, ((0, 0), (0, SIDE - width))), -REACH, axis=1)
    return pl.pallas_call(
        bands_kernel,
        out_shape=jax.ShapeDtypeStruct((filters, SIDE, SIDE), jnp.bfloat16),
        grid=(filters,),
        in_specs=[pl.BlockSpec((1, 1, SIDE), lambda f: (f, 0, 0))],
        out_specs=pl.BlockSpec((None, SIDE, SIDE), lambda f: (f, 0, 0)),
        compiler_params=pltpu.CompilerParams(vmem_limit_bytes=16 * MIB),
    )(first_rows.reshape(filters, 1, SIDE))


def warp_kernel(steps, where, meta, *refs):
    cands, (warps, out), scratch = refs[:12], refs[12:14], refs[14:]
    picks, tile, acc, sems = scratch
    z, y, odd = where[0], where[1], where[2]
    count = jnp.int32(0)
    for n, step in enumerate(steps):
        for t in range(TILES):
            for k in range(PER_TILE):
                far_y = (y + step) % RING
                at = t * PER_TILE + k
                q = meta[z * RING + far_y, at]
                owner = (q // TILES) % CHUNKS
                picks[0, count] = (
                    q // (TILES * CHUNKS) * (RING * TILES)
                    + ((owner // RING - z + RING) % RING) * TILES
                    + q % TILES
                )
                picks[1, count] = meta[z * RING + far_y, TILES * PER_TILE + at]
                picks[2, count] = meta[z * RING + far_y, 2 * TILES * PER_TILE + at]
                picks[3, count] = n * TILES + t
                count = count + (owner % RING == y).astype(jnp.int32)

    def copy(slot, source):
        return pltpu.make_async_copy(source, tile.at[slot], sems.at[slot])

    def start(i, slot):
        source = picks[0, i]
        for dz in range(RING):
            for local in range(TILES):
                at = 3 + local if dz == 2 else {0: 0, 3: 1, 1: 2}[dz]
                row = 0 if dz == 2 else local
                here = dz * TILES + local

                @pl.when(source == here)
                def _():
                    copy(slot, cands[at].at[row]).start()

                following = source == RING * TILES + here
                if dz % 2 == 0:

                    @pl.when(following)
                    def _():
                        copy(slot, cands[5 + at].at[row]).start()

                else:

                    @pl.when(following & (odd == 0))
                    def _():
                        copy(slot, cands[5 + at].at[row]).start()

                    @pl.when(following & (odd == 1))
                    def _():
                        copy(slot, cands[9 + at].at[row]).start()

    for i in range(DEEP - 1):

        @pl.when(i < count)
        def _():
            start(i, i)

    acc[...] = jnp.zeros_like(acc)

    def body(i, carry):
        slot = lax.rem(i, DEEP)
        copy(slot, cands[0].at[0]).wait()

        @pl.when(i + DEEP - 1 < count)
        def _():
            start(i + DEEP - 1, lax.rem(i + DEEP - 1, DEEP))

        inner = jnp.dot(warps[picks[1, i]], tile[slot], preferred_element_type=jnp.float32)
        piece = lax.dot_general(
            inner.astype(jnp.bfloat16),
            warps[picks[2, i]],
            (((1,), (1,)), ((), ())),
            preferred_element_type=jnp.float32,
        )
        target = picks[3, i]
        acc[target] = acc[target] + piece
        return carry

    lax.fori_loop(0, count, body, 0)
    out[...] = acc[...].astype(jnp.bfloat16)


def warp_partials(steps, where, meta, cands, warps):
    rows = len(steps) * TILES
    anywhere = pl.BlockSpec(memory_space=pl.ANY)
    scalars = pl.BlockSpec(memory_space=pltpu.SMEM)
    return pl.pallas_call(
        functools.partial(warp_kernel, steps),
        out_shape=jax.ShapeDtypeStruct((rows, SIDE, SIDE), jnp.bfloat16),
        in_specs=[scalars, scalars]
        + [anywhere] * len(cands)
        + [pl.BlockSpec(memory_space=pltpu.VMEM)],
        out_specs=pl.BlockSpec(memory_space=pltpu.VMEM),
        scratch_shapes=[
            pltpu.SMEM((4, rows * PER_TILE + 1), jnp.int32),
            pltpu.VMEM((DEEP, SIDE, SIDE), jnp.bfloat16),
            pltpu.VMEM((rows, SIDE, SIDE), jnp.float32),
            pltpu.SemaphoreType.DMA((DEEP,)),
        ],
        compiler_params=pltpu.CompilerParams(vmem_limit_bytes=28 * MIB),
        cost_estimate=pl.CostEstimate(
            flops=rows * 4 * SIDE**3, bytes_accessed=rows * 4 * SIDE**2 * 2, transcendentals=0
        ),
    )(where, meta, *cands, warps)


def match_kernel(picks, coef, bands, *refs):
    parts, (science, out, model) = refs[:6], refs[6:]
    ui = (2.0 * lax.broadcasted_iota(jnp.int32, (SIDE, 1), 0).astype(jnp.float32) + 1.0) / SIDE - 1.0
    uj = (2.0 * lax.broadcasted_iota(jnp.int32, (1, SIDE), 1).astype(jnp.float32) + 1.0) / SIDE - 1.0
    for t in range(TILES):
        first, second, third = parts[3 * t : 3 * t + 3]
        total = first[...].astype(jnp.float32) + second[...].astype(jnp.float32)
        warped = (total + third[...].astype(jnp.float32)).astype(jnp.bfloat16)
        for b in range(BASES):
            half = jnp.dot(bands[picks[0, t, b]], warped, preferred_element_type=jnp.float32)
            conv = lax.dot_general(
                half.astype(jnp.bfloat16),
                bands[picks[1, t, b]],
                (((1,), (1,)), ((), ())),
                preferred_element_type=jnp.float32,
            )
            term = (coef[t, b, 0] + coef[t, b, 1] * ui + coef[t, b, 2] * uj) * conv
            if b == 0:
                model[...] = term
            elif b < BASES - 1:
                model[...] += term
            else:
                left = science[t].astype(jnp.float32) - (model[...] + term)
                out[t] = left.astype(jnp.bfloat16)


def match(rows, cols, coef, bands, parts, science):
    whole = pl.BlockSpec(memory_space=pltpu.VMEM)
    scalars = pl.BlockSpec(memory_space=pltpu.SMEM)
    return pl.pallas_call(
        match_kernel,
        out_shape=jax.ShapeDtypeStruct((TILES, SIDE, SIDE), jnp.bfloat16),
        in_specs=[scalars, scalars] + [whole] * 8,
        out_specs=whole,
        scratch_shapes=[pltpu.VMEM((SIDE, SIDE), jnp.float32)],
        compiler_params=pltpu.CompilerParams(vmem_limit_bytes=28 * MIB),
        cost_estimate=pl.CostEstimate(
            flops=TILES * BASES * 4 * SIDE**3,
            bytes_accessed=(8 + 5) * SIDE**2 * 2,
            transcendentals=0,
        ),
    )(jnp.stack([rows, cols]), coef, bands, *parts, science)


def compose_kernel(level, target, place_in, chunks, out, sems):
    copies = [
        pltpu.make_async_copy(
            chunks.at[d], out.at[target[d] * level + place_in[d]], sems.at[d]
        )
        for d in range(CHUNKS)
    ]
    for copy in copies:
        copy.start()
    for copy in copies:
        copy.wait()


def compose(level, target, place_in, chunks):
    scalars = pl.BlockSpec(memory_space=pltpu.SMEM)
    return pl.pallas_call(
        functools.partial(compose_kernel, level),
        out_shape=jax.ShapeDtypeStruct((CHUNKS * level, CHUNK, SIDE), jnp.bfloat16),
        in_specs=[scalars, scalars, pl.BlockSpec(memory_space=pltpu.VMEM)],
        out_specs=pl.BlockSpec(memory_space=pl.ANY),
        scratch_shapes=[pltpu.SemaphoreType.DMA((CHUNKS,))],
        compiler_params=pltpu.CompilerParams(vmem_limit_bytes=16 * MIB),
    )(target, place_in, chunks)


def put_kernel(where, target, place_in, side, arrived, blank, out, tiles, sems):
    me = where[0] * RING + where[1]

    def loads(d, t):
        source = arrived.at[pl.ds(t * PER_CHUNK, PER_CHUNK), place_in[d]]
        at = d * TILES + t
        return pltpu.make_async_copy(source, tiles.at[at], sems.at[0, at])

    def stores(d, t):
        at = d * TILES + t
        goal = out.at[pl.ds((d * TILES + side[d, t]) * PER_CHUNK, PER_CHUNK)]
        return pltpu.make_async_copy(tiles.at[at], goal, sems.at[1, at])

    for d in range(CHUNKS):

        @pl.when(target[d] == me)
        def _():
            for t in range(TILES):
                loads(d, t).start()

    for d in range(CHUNKS):

        @pl.when(target[d] == me)
        def _():
            for t in range(TILES):
                loads(d, t).wait()
                stores(d, t).start()

    for d in range(CHUNKS):

        @pl.when(target[d] == me)
        def _():
            for t in range(TILES):
                stores(d, t).wait()


def put(where, target, place_in, side, arrived, blank):
    anywhere = pl.BlockSpec(memory_space=pl.ANY)
    scalars = pl.BlockSpec(memory_space=pltpu.SMEM)
    return pl.pallas_call(
        put_kernel,
        out_shape=jax.ShapeDtypeStruct(blank.shape, blank.dtype),
        in_specs=[scalars] * 4 + [anywhere] * 2,
        out_specs=anywhere,
        scratch_shapes=[
            pltpu.VMEM((CHUNKS * TILES, PER_CHUNK, CHUNK, SIDE), jnp.bfloat16),
            pltpu.SemaphoreType.DMA((2, CHUNKS * TILES)),
        ],
        input_output_aliases={5: 0},
        compiler_params=pltpu.CompilerParams(vmem_limit_bytes=24 * MIB),
    )(where, target, place_in, side, arrived, blank)


def blank_kernel(out, zeros, sems):
    zeros[...] = jnp.zeros_like(zeros)
    copies = [
        pltpu.make_async_copy(
            zeros, out.at[pl.ds(n * PER_CHUNK, PER_CHUNK)], sems.at[n]
        )
        for n in range(CHUNKS * TILES)
    ]
    for copy in copies:
        copy.start()
    for copy in copies:
        copy.wait()


def make_blank():
    return pl.pallas_call(
        blank_kernel,
        out_shape=jax.ShapeDtypeStruct((CHUNKS * CHUNKS, CHUNK, SIDE), jnp.bfloat16),
        out_specs=pl.BlockSpec(memory_space=pl.ANY),
        scratch_shapes=[
            pltpu.VMEM((PER_CHUNK, CHUNK, SIDE), jnp.bfloat16),
            pltpu.SemaphoreType.DMA((CHUNKS * TILES,)),
        ],
        compiler_params=pltpu.CompilerParams(vmem_limit_bytes=16 * MIB),
    )()


def shards(
    templates,
    science,
    intersection,
    row_warp,
    col_warp,
    warps,
    taps,
    basis_row,
    basis_col,
    coef,
    home,
):
    me = lax.axis_index("det")
    odd = lax.axis_index("sky") % 2
    where = jnp.stack([me // RING, me % RING, odd]).astype(jnp.int32)

    with jax.named_scope("gather_templates"):
        following = next_patch(templates)
        before = along(templates, "z", 1)
        after = along(templates, "z", -1)

    with jax.named_scope("spread_tables"):
        table = jnp.concatenate(
            [intersection.reshape(-1), row_warp.reshape(-1), col_warp.reshape(-1), home]
        )
        meta = all_rows(table, "det")
        homes = meta[:, 3 * TILES * PER_TILE :]
        target = homes[:, 0] // TILES
        side = homes % TILES
        same = (target[:, None] == target[None, :]).astype(jnp.int32)
        place_in = jnp.sum(jnp.tril(same, -1), axis=1)
        busiest = all_rows(jnp.max(jnp.sum(same, axis=1)).reshape(1), "sky")
        level = jnp.sum((jnp.max(busiest) > jnp.array(LEVELS[:-1])).astype(jnp.int32))

    with jax.named_scope("gather_templates"):
        before, after, following, meta, level = together(before, after, following, meta, level)
        far = (along(before[:1], "z", 1), along(after[1:], "z", -1))
        blank = make_blank()
        far_before, far_after, blank = together(*far, blank)
        cands = (
            templates,
            before,
            after,
            far_before,
            far_after,
            following,
            next_patch(before, 0, 2),
            next_patch(after, 0, 2),
            next_patch(far_before),
            next_patch(far_after),
            along_odd(following, 1),
            along_odd(following, -1),
        )

    with jax.named_scope("warp"):
        opposite = warp_partials((2,), where, meta, cands, warps)
        nearer = warp_partials((0, 1, 3), where, meta, cands, warps)

    with jax.named_scope("sum_partials"):
        taps, _ = together(taps, nearer)
        bands = make_bands(taps)
        up = along(opposite[0], "y", 1)
        down = along(opposite[1], "y", -1)

        def plus(a, b):
            return (a.astype(jnp.float32) + b.astype(jnp.float32)).astype(jnp.bfloat16)

        parts = (
            nearer[0],
            along(plus(nearer[2], up), "y", 1),
            along(nearer[4], "y", -1),
            nearer[1],
            along(nearer[3], "y", 1),
            along(plus(nearer[5], down), "y", -1),
        )

    with jax.named_scope("match"):
        diffs = match(basis_row, basis_col, coef, bands, parts, science)

    with jax.named_scope("spread_differences"):
        chunks = lax.all_to_all(
            diffs.reshape(CHUNKS, CHUNK, SIDE), "det", split_axis=0, concat_axis=0, tiled=True
        )

    def send(slots):
        def branch(chunks, blank):
            leaving = compose(slots, target, place_in, chunks)
            arrived = lax.all_to_all(leaving, "det", split_axis=0, concat_axis=0, tiled=True)
            arrived = arrived.reshape(CHUNKS, slots, CHUNK, SIDE)
            return put(where, target, place_in, side, arrived, blank)

        return branch

    with jax.named_scope("give_back"):
        full = lax.switch(level, [send(slots) for slots in LEVELS], chunks, blank)
    return full.reshape(CHUNKS * TILES, SIDE, SIDE)


def solution(mesh):
    placed = (
        P(("sky", "det"), None, None),
        P(("sky", "det"), None, None),
        P(("sky", "det"), None),
        P(("sky", "det"), None),
        P(("sky", "det"), None),
        P(),
        P(),
        P(("sky", "det"), None),
        P(("sky", "det"), None),
        P(("sky", "det"), None, None),
        P(("sky", "det")),
    )
    return jax.shard_map(
        shards, mesh=mesh, in_specs=placed, out_specs=P(("sky", "det"), None, None), check_vma=False
    )
```

```python
import functools
import itertools

import jax
import jax.numpy as jnp
from jax import lax
from jax.experimental import pallas as pl
from jax.experimental.pallas import tpu as pltpu
from jax.sharding import PartitionSpec as P

SIDE = 512
RING = 4
TILES = 2
PER_TILE = 4
BASES = 5
REACH = 10
CHUNKS = RING * RING
CHUNK = TILES * SIDE // CHUNKS
PER_CHUNK = CHUNKS // TILES
BANK = 8
LEVELS = (3, 4, 5, 6, 8, 16)
DEEP = 4
MIB = 1024 * 1024


def place(z, y):
    return (z % RING) * RING + y % RING


def hop(block, dz, dy):
    route = [
        (place(z, y), place(z + dz, y + dy)) for z in range(RING) for y in range(RING)
    ]
    return lax.ppermute(block, "det", route)


def along(block, axis, step):
    return hop(block, step, 0) if axis == "z" else hop(block, 0, step)


def next_patch(block):
    count = lax.axis_size("sky")
    return lax.ppermute(block, "sky", [((i + 1) % count, i) for i in range(count)])


def all_rows(row, axis):
    copies = jnp.broadcast_to(row, (lax.axis_size(axis), *row.shape))
    return lax.all_to_all(copies, axis, split_axis=0, concat_axis=0, tiled=True)


def together(*arrays):
    return lax.optimization_barrier(arrays)


def bands_kernel(taps, out):
    shape = (SIDE, SIDE)
    rows = lax.broadcasted_iota(jnp.int32, shape, 0)
    cols = lax.broadcasted_iota(jnp.int32, shape, 1)
    rolled = pltpu.roll(jnp.broadcast_to(taps[0], shape), 0, 1, stride=1, stride_axis=0)
    out[...] = jnp.where(jnp.abs(cols - rows) <= REACH, rolled, 0.0).astype(jnp.bfloat16)


def make_bands(taps):
    filters, width = taps.shape
    assert width == 2 * REACH + 1
    first_rows = jnp.roll(jnp.pad(taps, ((0, 0), (0, SIDE - width))), -REACH, axis=1)
    return pl.pallas_call(
        bands_kernel,
        out_shape=jax.ShapeDtypeStruct((filters, SIDE, SIDE), jnp.bfloat16),
        grid=(filters,),
        in_specs=[pl.BlockSpec((1, 1, SIDE), lambda f: (f, 0, 0))],
        out_specs=pl.BlockSpec((None, SIDE, SIDE), lambda f: (f, 0, 0)),
        compiler_params=pltpu.CompilerParams(vmem_limit_bytes=16 * MIB),
    )(first_rows.reshape(filters, 1, SIDE))


def warp_kernel(steps, where, meta, *refs):
    rows = len(steps) * TILES
    cands, warps, outs, scratch = refs[:14], refs[14], refs[15 : 15 + rows], refs[15 + rows :]
    picks, ready, tile, bank, acc, sems, bank_sems = scratch
    z, y = where[0], where[1]
    count = jnp.int32(0)
    for n, step in enumerate(steps):
        for t in range(TILES):
            for k in range(PER_TILE):
                far_y = (y + step) % RING
                row = z * RING + far_y
                q = meta[row, t, k]
                owner = (q // TILES) % CHUNKS
                picks[0, count] = (
                    q // (TILES * CHUNKS) * (RING * TILES)
                    + ((owner // RING - z + RING) % RING) * TILES
                    + q % TILES
                )
                picks[1, count] = meta[row, t, PER_TILE + k]
                picks[2, count] = meta[row, t, 2 * PER_TILE + k]
                picks[3, count] = n * TILES + t
                count = count + (owner % RING == y).astype(jnp.int32)

    def bank_copy(n):
        return pltpu.make_async_copy(warps.at[n], bank.at[n], bank_sems.at[n])

    def need(n):
        @pl.when(ready[n] == 0)
        def _():
            bank_copy(n).wait()
            ready[n] = 1

    def copy(slot, source):
        return pltpu.make_async_copy(source, tile.at[slot], sems.at[slot])

    def start(i, slot):
        source = picks[0, i]
        for which in range(2):
            for dz, local in itertools.product(range(RING), range(TILES)):
                if dz == 0:
                    block = cands[7 * which].at[local]
                else:
                    block = cands[7 * which + {3: 1, 1: 3, 2: 5}[dz] + local]

                @pl.when(source == (which * RING + dz) * TILES + local)
                def _():
                    copy(slot, block).start()

    for i in range(DEEP - 1):

        @pl.when(i < count)
        def _():
            start(i, i)

    for n in range(BANK):
        bank_copy(n).start()
        ready[n] = 0

    acc[...] = jnp.zeros_like(acc)

    def body(i, carry):
        slot = lax.rem(i, DEEP)
        copy(slot, cands[0].at[0]).wait()

        @pl.when(i + DEEP - 1 < count)
        def _():
            start(i + DEEP - 1, lax.rem(i + DEEP - 1, DEEP))

        need(picks[1, i])
        need(picks[2, i])
        inner = jnp.dot(bank[picks[1, i]], tile[slot], preferred_element_type=jnp.float32)
        piece = lax.dot_general(
            inner.astype(jnp.bfloat16),
            bank[picks[2, i]],
            (((1,), (1,)), ((), ())),
            preferred_element_type=jnp.float32,
        )
        target = picks[3, i]
        acc[target] = acc[target] + piece
        return carry

    lax.fori_loop(0, count, body, 0)
    for n in range(BANK):
        need(n)
    for n, out in enumerate(outs):
        out[...] = acc[n].astype(jnp.bfloat16)


def warp_partials(steps, where, meta, cands, warps):
    rows = len(steps) * TILES
    scalars = pl.BlockSpec(memory_space=pltpu.SMEM)
    return pl.pallas_call(
        functools.partial(warp_kernel, steps),
        out_shape=[jax.ShapeDtypeStruct((SIDE, SIDE), jnp.bfloat16)] * rows,
        in_specs=[scalars, scalars]
        + [pl.BlockSpec(memory_space=pltpu.HBM)] * (len(cands) + 1),
        out_specs=[pl.BlockSpec(memory_space=pltpu.VMEM)] * rows,
        scratch_shapes=[
            pltpu.SMEM((4, rows * PER_TILE + 1), jnp.int32),
            pltpu.SMEM((BANK,), jnp.int32),
            pltpu.VMEM((DEEP, SIDE, SIDE), jnp.bfloat16),
            pltpu.VMEM((BANK, SIDE, SIDE), jnp.bfloat16),
            pltpu.VMEM((rows, SIDE, SIDE), jnp.float32),
            pltpu.SemaphoreType.DMA((DEEP,)),
            pltpu.SemaphoreType.DMA((BANK,)),
        ],
        compiler_params=pltpu.CompilerParams(vmem_limit_bytes=28 * MIB),
        cost_estimate=pl.CostEstimate(
            flops=rows * 4 * SIDE**3, bytes_accessed=rows * 4 * SIDE**2 * 2, transcendentals=0
        ),
    )(where, meta, *[pltpu.with_memory_space_constraint(x, pltpu.HBM) for x in (*cands, warps)])


def match_kernel(picks, coef, bands, *refs):
    parts, (science, out, model) = refs[:6], refs[6:]
    ui = (2.0 * lax.broadcasted_iota(jnp.int32, (SIDE, 1), 0).astype(jnp.float32) + 1.0) / SIDE - 1.0
    uj = (2.0 * lax.broadcasted_iota(jnp.int32, (1, SIDE), 1).astype(jnp.float32) + 1.0) / SIDE - 1.0
    for t in range(TILES):
        first, second, third = parts[3 * t : 3 * t + 3]
        total = first[...].astype(jnp.float32) + second[...].astype(jnp.float32)
        warped = (total + third[...].astype(jnp.float32)).astype(jnp.bfloat16)
        for b in range(BASES):
            half = jnp.dot(bands[picks[0, t, b]], warped, preferred_element_type=jnp.float32)
            conv = lax.dot_general(
                half.astype(jnp.bfloat16),
                bands[picks[1, t, b]],
                (((1,), (1,)), ((), ())),
                preferred_element_type=jnp.float32,
            )
            term = (coef[t, b, 0] + coef[t, b, 1] * ui + coef[t, b, 2] * uj) * conv
            if b == 0:
                model[...] = term
            elif b < BASES - 1:
                model[...] += term
            else:
                left = science[t].astype(jnp.float32) - (model[...] + term)
                out[t] = left.astype(jnp.bfloat16)


def match(rows, cols, coef, bands, parts, science):
    whole = pl.BlockSpec(memory_space=pltpu.VMEM)
    scalars = pl.BlockSpec(memory_space=pltpu.SMEM)
    return pl.pallas_call(
        match_kernel,
        out_shape=jax.ShapeDtypeStruct((TILES, SIDE, SIDE), jnp.bfloat16),
        in_specs=[scalars, scalars] + [whole] * 8,
        out_specs=whole,
        scratch_shapes=[pltpu.VMEM((SIDE, SIDE), jnp.float32)],
        compiler_params=pltpu.CompilerParams(vmem_limit_bytes=28 * MIB),
        cost_estimate=pl.CostEstimate(
            flops=TILES * BASES * 4 * SIDE**3,
            bytes_accessed=(8 + 5) * SIDE**2 * 2,
            transcendentals=0,
        ),
    )(jnp.stack([rows, cols]), coef, bands, *parts, science)


def compose_kernel(level, target, place_in, chunks, out, sems):
    copies = [
        pltpu.make_async_copy(
            chunks.at[d], out.at[target[d] * level + place_in[d]], sems.at[d]
        )
        for d in range(CHUNKS)
    ]
    for copy in copies:
        copy.start()
    for copy in copies:
        copy.wait()


def compose(level, target, place_in, chunks):
    scalars = pl.BlockSpec(memory_space=pltpu.SMEM)
    return pl.pallas_call(
        functools.partial(compose_kernel, level),
        out_shape=pltpu.HBM((CHUNKS * level, CHUNK, SIDE), jnp.bfloat16),
        in_specs=[scalars, scalars, pl.BlockSpec(memory_space=pltpu.VMEM)],
        out_specs=pl.BlockSpec(memory_space=pltpu.HBM),
        scratch_shapes=[pltpu.SemaphoreType.DMA((CHUNKS,))],
        compiler_params=pltpu.CompilerParams(vmem_limit_bytes=16 * MIB),
    )(target, place_in, chunks)


def put_kernel(where, target, place_in, side, arrived, blank, out, tiles, sems):
    me = where[0] * RING + where[1]

    def loads(d, t):
        source = arrived.at[pl.ds(t * PER_CHUNK, PER_CHUNK), place_in[d]]
        at = d * TILES + t
        return pltpu.make_async_copy(source, tiles.at[at], sems.at[0, at])

    def stores(d, t):
        at = d * TILES + t
        goal = out.at[pl.ds((d * TILES + side[d, t]) * PER_CHUNK, PER_CHUNK)]
        return pltpu.make_async_copy(tiles.at[at], goal, sems.at[1, at])

    for d in range(CHUNKS):

        @pl.when(target[d] == me)
        def _():
            for t in range(TILES):
                loads(d, t).start()

    for d in range(CHUNKS):

        @pl.when(target[d] == me)
        def _():
            for t in range(TILES):
                loads(d, t).wait()
                stores(d, t).start()

    for d in range(CHUNKS):

        @pl.when(target[d] == me)
        def _():
            for t in range(TILES):
                stores(d, t).wait()


def put(where, target, place_in, side, arrived, blank):
    anywhere = pl.BlockSpec(memory_space=pltpu.HBM)
    scalars = pl.BlockSpec(memory_space=pltpu.SMEM)
    return pl.pallas_call(
        put_kernel,
        out_shape=jax.ShapeDtypeStruct(blank.shape, blank.dtype),
        in_specs=[scalars] * 4 + [anywhere] * 2,
        out_specs=anywhere,
        scratch_shapes=[
            pltpu.VMEM((CHUNKS * TILES, PER_CHUNK, CHUNK, SIDE), jnp.bfloat16),
            pltpu.SemaphoreType.DMA((2, CHUNKS * TILES)),
        ],
        input_output_aliases={5: 0},
        compiler_params=pltpu.CompilerParams(vmem_limit_bytes=24 * MIB),
    )(where, target, place_in, side, arrived, blank)


def blank_kernel(out, zeros, sems):
    zeros[...] = jnp.zeros_like(zeros)
    copies = [
        pltpu.make_async_copy(
            zeros, out.at[pl.ds(n * PER_CHUNK, PER_CHUNK)], sems.at[n]
        )
        for n in range(CHUNKS * TILES)
    ]
    for copy in copies:
        copy.start()
    for copy in copies:
        copy.wait()


def make_blank():
    return pl.pallas_call(
        blank_kernel,
        out_shape=pltpu.HBM((CHUNKS * CHUNKS, CHUNK, SIDE), jnp.bfloat16),
        out_specs=pl.BlockSpec(memory_space=pltpu.HBM),
        scratch_shapes=[
            pltpu.VMEM((PER_CHUNK, CHUNK, SIDE), jnp.bfloat16),
            pltpu.SemaphoreType.DMA((CHUNKS * TILES,)),
        ],
        compiler_params=pltpu.CompilerParams(vmem_limit_bytes=16 * MIB),
    )()


def shards(
    templates,
    science,
    intersection,
    row_warp,
    col_warp,
    warps,
    taps,
    basis_row,
    basis_col,
    coef,
    home,
):
    me = lax.axis_index("det")
    where = jnp.stack([me // RING, me % RING]).astype(jnp.int32)

    with jax.named_scope("gather_templates"):
        tiles = (templates[0], templates[1])
        following = next_patch(templates)
        before = [along(tiles[0], "z", 1), None]
        after = [None, along(tiles[1], "z", -1)]
        before[1] = along(tiles[1], "z", 1)
        after[0] = along(tiles[0], "z", -1)
        far = [along(before[0], "z", 1), along(after[1], "z", -1)]
        blank, _ = together(make_blank(), far[0])
        here = (templates, *before, *after, *far)
        there = (following,) + tuple(next_patch(block) for block in here[1:])

    with jax.named_scope("spread_tables"):
        table = jnp.concatenate([intersection, row_warp, col_warp, home[:, None]], axis=1)
        table, _, _ = together(table, *far)
        meta = all_rows(table, "det")
        homes = meta[:, :, 3 * PER_TILE]
        target = homes[:, 0] // TILES
        side = homes % TILES
        same = (target[:, None] == target[None, :]).astype(jnp.int32)
        place_in = jnp.sum(jnp.tril(same, -1), axis=1)
        busiest = jnp.max(jnp.sum(same, axis=1)).reshape(1)

    with jax.named_scope("warp"):
        opposite = warp_partials((2,), where, meta, here + there, warps)
        nearer = warp_partials((0, 1, 3), where, meta, here + there, warps)

    with jax.named_scope("sum_partials"):
        busiest, _ = together(busiest, nearer[0])
        up = along(opposite[0], "y", 1)
        down = along(opposite[1], "y", -1)

        def plus(a, b):
            return (a.astype(jnp.float32) + b.astype(jnp.float32)).astype(jnp.bfloat16)

        parts = (
            nearer[0],
            along(plus(nearer[2], up), "y", 1),
            along(nearer[4], "y", -1),
            nearer[1],
            along(nearer[3], "y", 1),
            along(plus(nearer[5], down), "y", -1),
        )

    with jax.named_scope("busiest_home"):
        busiest = all_rows(busiest, "sky")
        level = jnp.sum((jnp.max(busiest) > jnp.array(LEVELS[:-1])).astype(jnp.int32))
        taps, level = together(taps, level)
        bands = make_bands(taps)

    with jax.named_scope("match"):
        diffs = match(basis_row, basis_col, coef, bands, parts, science)

    with jax.named_scope("spread_differences"):
        chunks = lax.all_to_all(
            diffs.reshape(CHUNKS, CHUNK, SIDE), "det", split_axis=0, concat_axis=0, tiled=True
        )

    def send(slots):
        def branch(chunks, blank):
            leaving = compose(slots, target, place_in, chunks)
            arrived = lax.all_to_all(leaving, "det", split_axis=0, concat_axis=0, tiled=True)
            arrived = arrived.reshape(CHUNKS, slots, CHUNK, SIDE)
            return put(where, target, place_in, side, arrived, blank)

        return branch

    with jax.named_scope("give_back"):
        full = lax.switch(level, [send(slots) for slots in LEVELS], chunks, blank)
    return full.reshape(CHUNKS * TILES, SIDE, SIDE)


def solution(mesh):
    placed = (
        P(("sky", "det"), None, None),
        P(("sky", "det"), None, None),
        P(("sky", "det"), None),
        P(("sky", "det"), None),
        P(("sky", "det"), None),
        P(),
        P(),
        P(("sky", "det"), None),
        P(("sky", "det"), None),
        P(("sky", "det"), None, None),
        P(("sky", "det")),
    )
    return jax.shard_map(
        shards, mesh=mesh, in_specs=placed, out_specs=P(("sky", "det"), None, None), check_vma=False
    )
```

```python
import functools
import itertools

import jax
import jax.numpy as jnp
from jax import lax
from jax.experimental import pallas as pl
from jax.experimental.pallas import tpu as pltpu
from jax.sharding import PartitionSpec as P

SIDE = 512
RING = 4
TILES = 2
PER_TILE = 4
BASES = 5
REACH = 10
CHUNKS = RING * RING
QUARTER = SIDE // RING
BANK = 8
MOST, MORE, REST = (0, 4), (4, 5), (5, CHUNKS)
DEEP = 4
MIB = 1024 * 1024


def place(z, y):
    return (z % RING) * RING + y % RING


def hop(block, dz, dy):
    route = [
        (place(z, y), place(z + dz, y + dy)) for z in range(RING) for y in range(RING)
    ]
    return lax.ppermute(block, "det", route)


def along(block, axis, step):
    return hop(block, step, 0) if axis == "z" else hop(block, 0, step)


def next_patch(block):
    count = lax.axis_size("sky")
    return lax.ppermute(block, "sky", [((i + 1) % count, i) for i in range(count)])


def all_rows(row, axis):
    copies = jnp.broadcast_to(row, (lax.axis_size(axis), *row.shape))
    return lax.all_to_all(copies, axis, split_axis=0, concat_axis=0, tiled=True)


def together(*arrays):
    return lax.optimization_barrier(arrays)


def bands_kernel(taps, out):
    shape = (SIDE, SIDE)
    rows = lax.broadcasted_iota(jnp.int32, shape, 0)
    cols = lax.broadcasted_iota(jnp.int32, shape, 1)
    rolled = pltpu.roll(jnp.broadcast_to(taps[0], shape), 0, 1, stride=1, stride_axis=0)
    out[...] = jnp.where(jnp.abs(cols - rows) <= REACH, rolled, 0.0).astype(jnp.bfloat16)


def make_bands(taps):
    filters, width = taps.shape
    assert width == 2 * REACH + 1
    first_rows = jnp.roll(jnp.pad(taps, ((0, 0), (0, SIDE - width))), -REACH, axis=1)
    return pl.pallas_call(
        bands_kernel,
        out_shape=jax.ShapeDtypeStruct((filters, SIDE, SIDE), jnp.bfloat16),
        grid=(filters,),
        in_specs=[pl.BlockSpec((1, 1, SIDE), lambda f: (f, 0, 0))],
        out_specs=pl.BlockSpec((None, SIDE, SIDE), lambda f: (f, 0, 0)),
        compiler_params=pltpu.CompilerParams(vmem_limit_bytes=16 * MIB),
    )(first_rows.reshape(filters, 1, SIDE))


def warp_kernel(steps, where, meta, *refs):
    rows = len(steps) * TILES
    cands, warps, outs, scratch = refs[:14], refs[14], refs[15 : 15 + rows], refs[15 + rows :]
    picks, ready, tile, bank, acc, sems, bank_sems = scratch
    z, y = where[0], where[1]
    count = jnp.int32(0)
    for n, step in enumerate(steps):
        for t in range(TILES):
            for k in range(PER_TILE):
                far_y = (y + step) % RING
                row = z * RING + far_y
                q = meta[row, t, k]
                owner = (q // TILES) % CHUNKS
                picks[0, count] = (
                    q // (TILES * CHUNKS) * (RING * TILES)
                    + ((owner // RING - z + RING) % RING) * TILES
                    + q % TILES
                )
                picks[1, count] = meta[row, t, PER_TILE + k]
                picks[2, count] = meta[row, t, 2 * PER_TILE + k]
                picks[3, count] = n * TILES + t
                count = count + (owner % RING == y).astype(jnp.int32)

    def bank_copy(n):
        return pltpu.make_async_copy(warps.at[n], bank.at[n], bank_sems.at[n])

    def need(n):
        @pl.when(ready[n] == 0)
        def _():
            bank_copy(n).wait()
            ready[n] = 1

    def copy(slot, source):
        return pltpu.make_async_copy(source, tile.at[slot], sems.at[slot])

    def start(i, slot):
        source = picks[0, i]
        for which in range(2):
            for dz, local in itertools.product(range(RING), range(TILES)):
                if dz == 0:
                    block = cands[7 * which].at[local]
                else:
                    block = cands[7 * which + {3: 1, 1: 3, 2: 5}[dz] + local]

                @pl.when(source == (which * RING + dz) * TILES + local)
                def _():
                    copy(slot, block).start()

    for i in range(DEEP - 1):

        @pl.when(i < count)
        def _():
            start(i, i)

    for n in range(BANK):
        bank_copy(n).start()
        ready[n] = 0

    acc[...] = jnp.zeros_like(acc)

    def body(i, carry):
        slot = lax.rem(i, DEEP)
        copy(slot, cands[0].at[0]).wait()

        @pl.when(i + DEEP - 1 < count)
        def _():
            start(i + DEEP - 1, lax.rem(i + DEEP - 1, DEEP))

        need(picks[1, i])
        need(picks[2, i])
        inner = jnp.dot(bank[picks[1, i]], tile[slot], preferred_element_type=jnp.float32)
        piece = lax.dot_general(
            inner.astype(jnp.bfloat16),
            bank[picks[2, i]],
            (((1,), (1,)), ((), ())),
            preferred_element_type=jnp.float32,
        )
        target = picks[3, i]
        acc[target] = acc[target] + piece
        return carry

    lax.fori_loop(0, count, body, 0)
    for n in range(BANK):
        need(n)
    for n, out in enumerate(outs):
        out[...] = acc[n].astype(jnp.bfloat16)


def warp_partials(steps, where, meta, cands, warps):
    rows = len(steps) * TILES
    scalars = pl.BlockSpec(memory_space=pltpu.SMEM)
    return pl.pallas_call(
        functools.partial(warp_kernel, steps),
        out_shape=[jax.ShapeDtypeStruct((SIDE, SIDE), jnp.bfloat16)] * rows,
        in_specs=[scalars, scalars]
        + [pl.BlockSpec(memory_space=pltpu.HBM)] * (len(cands) + 1),
        out_specs=[pl.BlockSpec(memory_space=pltpu.VMEM)] * rows,
        scratch_shapes=[
            pltpu.SMEM((4, rows * PER_TILE + 1), jnp.int32),
            pltpu.SMEM((BANK,), jnp.int32),
            pltpu.VMEM((DEEP, SIDE, SIDE), jnp.bfloat16),
            pltpu.VMEM((BANK, SIDE, SIDE), jnp.bfloat16),
            pltpu.VMEM((rows, SIDE, SIDE), jnp.float32),
            pltpu.SemaphoreType.DMA((DEEP,)),
            pltpu.SemaphoreType.DMA((BANK,)),
        ],
        compiler_params=pltpu.CompilerParams(vmem_limit_bytes=28 * MIB),
        cost_estimate=pl.CostEstimate(
            flops=rows * 4 * SIDE**3, bytes_accessed=rows * 4 * SIDE**2 * 2, transcendentals=0
        ),
    )(where, meta, *[pltpu.with_memory_space_constraint(x, pltpu.HBM) for x in (*cands, warps)])


def match_kernel(where, picks, coef, bands, *refs):
    parts, science, outs, (whole, model) = refs[:6], refs[6], refs[7:15], refs[15:]
    ui = (2.0 * lax.broadcasted_iota(jnp.int32, (SIDE, 1), 0).astype(jnp.float32) + 1.0) / SIDE - 1.0
    uj = (2.0 * lax.broadcasted_iota(jnp.int32, (1, SIDE), 1).astype(jnp.float32) + 1.0) / SIDE - 1.0
    for t in range(TILES):
        first, second, third = parts[3 * t : 3 * t + 3]
        total = first[...].astype(jnp.float32) + second[...].astype(jnp.float32)
        warped = (total + third[...].astype(jnp.float32)).astype(jnp.bfloat16)
        for b in range(BASES):
            half = jnp.dot(bands[picks[0, t, b]], warped, preferred_element_type=jnp.float32)
            conv = lax.dot_general(
                half.astype(jnp.bfloat16),
                bands[picks[1, t, b]],
                (((1,), (1,)), ((), ())),
                preferred_element_type=jnp.float32,
            )
            term = (coef[t, b, 0] + coef[t, b, 1] * ui + coef[t, b, 2] * uj) * conv
            if b == 0:
                model[...] = term
            elif b < BASES - 1:
                model[...] += term
            else:
                left = science[t].astype(jnp.float32) - (model[...] + term)
                whole[...] = left.astype(jnp.bfloat16)
        for k in range(RING):
            quarter = (where[1 - t] + k) % RING
            outs[t * RING + k][...] = whole[pl.ds(quarter * QUARTER, QUARTER)]


def match(where, rows, cols, coef, bands, parts, science):
    whole = pl.BlockSpec(memory_space=pltpu.VMEM)
    scalars = pl.BlockSpec(memory_space=pltpu.SMEM)
    return pl.pallas_call(
        match_kernel,
        out_shape=[jax.ShapeDtypeStruct((QUARTER, SIDE), jnp.bfloat16)] * (TILES * RING),
        in_specs=[scalars] * 3 + [whole] * 8,
        out_specs=[whole] * (TILES * RING),
        scratch_shapes=[
            pltpu.VMEM((SIDE, SIDE), jnp.bfloat16),
            pltpu.VMEM((SIDE, SIDE), jnp.float32),
        ],
        compiler_params=pltpu.CompilerParams(vmem_limit_bytes=28 * MIB),
        cost_estimate=pl.CostEstimate(
            flops=TILES * BASES * 4 * SIDE**3,
            bytes_accessed=(8 + 5) * SIDE**2 * 2,
            transcendentals=0,
        ),
    )(where, jnp.stack([rows, cols]), coef, bands, *parts, science)


def compose_kernel(spans, where, target, place_in, *refs):
    held, outs, sems = refs[:8], refs[8:-1], refs[-1]
    z, y = where[0], where[1]

    def each(t, j, action):
        def body(k, carry):
            source_z, source_y = (z - j, y - k) if t == 0 else (z - k, y - j)
            source = ((source_z + RING) % RING) * RING + (source_y + RING) % RING
            goal = target[source]
            if t == 0:
                live, step = goal // RING == z, (goal % RING - y + RING) % RING
            else:
                live, step = goal % RING == y, (goal // RING - z + RING) % RING
            slot = place_in[source]
            live = live & (slot >= spans[0][0]) & (slot < spans[-1][1])

            @pl.when(live)
            def _():
                action(t, j, k, step, slot)

            return carry

        lax.fori_loop(0, RING, body, 0)

    def copy(t, j, k, m, span, slot):
        goal = outs[(span * TILES + t) * RING + m].at[slot]
        n = (t * RING + j) * RING + k
        return pltpu.make_async_copy(held[t * RING + j].at[k], goal, sems.at[n])

    def begin(t, j, k, step, slot):
        for span, (low, high) in enumerate(spans):
            for m in range(RING):

                @pl.when((step == m) & (slot >= low) & (slot < high))
                def _():
                    copy(t, j, k, m, span, slot - low).start()

    def finish(t, j, k, step, slot):
        copy(t, j, k, 0, 0, 0).wait()

    for action in (begin, finish):
        for t, j in itertools.product(range(TILES), range(RING)):
            each(t, j, action)


def compose(spans, where, target, place_in, held):
    memory = pl.BlockSpec(memory_space=pltpu.VMEM)
    scalars = pl.BlockSpec(memory_space=pltpu.SMEM)
    shapes, specs = [], []
    for (low, high), _, m in itertools.product(spans, range(TILES), range(RING)):
        shape = (high - low, QUARTER, SIDE)
        stays = m == 0
        shapes.append(
            jax.ShapeDtypeStruct(shape, jnp.bfloat16) if stays else pltpu.HBM(shape, jnp.bfloat16)
        )
        specs.append(memory if stays else pl.BlockSpec(memory_space=pltpu.HBM))
    outs = pl.pallas_call(
        functools.partial(compose_kernel, spans),
        out_shape=shapes,
        in_specs=[scalars] * 3 + [memory] * len(held),
        out_specs=specs,
        scratch_shapes=[pltpu.SemaphoreType.DMA((TILES * CHUNKS,))],
        compiler_params=pltpu.CompilerParams(vmem_limit_bytes=16 * MIB),
    )(where, target, place_in, *held)
    width = TILES * RING
    return [outs[n * width : (n + 1) * width] for n in range(len(spans))]


def put_kernel(spans, where, target, place_in, side, *refs):
    arrived, (_, out, sems) = refs[:-3], refs[-3:]
    me = where[0] * RING + where[1]

    def copy(d, t, m, span, slot):
        quarter = (where[1 - t] - m + RING) % RING
        return pltpu.make_async_copy(
            arrived[(span * TILES + t) * RING + m].at[slot],
            out.at[d * TILES + side[d, t], pl.ds(quarter * QUARTER, QUARTER)],
            sems.at[d * TILES + t, m],
        )

    def begin(d):
        slot = place_in[d]
        for span, (low, high) in enumerate(spans):

            @pl.when((slot >= low) & (slot < high))
            def _():
                for t, m in itertools.product(range(TILES), range(RING)):
                    copy(d, t, m, span, slot - low).start()

    def finish(d):
        for t, m in itertools.product(range(TILES), range(RING)):
            copy(d, t, m, 0, 0).wait()

    for action in (begin, finish):

        def body(d, carry):
            slot = place_in[d]
            live = (target[d] == me) & (slot >= spans[0][0]) & (slot < spans[-1][1])

            @pl.when(live)
            def _():
                action(d)

            return carry

        lax.fori_loop(0, CHUNKS, body, 0)


def put(spans, where, target, place_in, side, arrived, blank):
    scalars = pl.BlockSpec(memory_space=pltpu.SMEM)
    arrays = [block for span in arrived for block in span]
    return pl.pallas_call(
        functools.partial(put_kernel, spans),
        out_shape=pltpu.HBM(blank.shape, blank.dtype),
        in_specs=[scalars] * 4
        + [pl.BlockSpec(memory_space=pltpu.VMEM)] * len(arrays)
        + [pl.BlockSpec(memory_space=pltpu.HBM)],
        out_specs=pl.BlockSpec(memory_space=pltpu.HBM),
        scratch_shapes=[pltpu.SemaphoreType.DMA((CHUNKS * TILES, RING))],
        input_output_aliases={4 + len(arrays): 0},
        compiler_params=pltpu.CompilerParams(vmem_limit_bytes=24 * MIB),
    )(where, target, place_in, side, *arrays, blank)


def blank_kernel(_, out, zeros, sems):
    zeros[...] = jnp.zeros_like(zeros)
    copies = [
        pltpu.make_async_copy(zeros, out.at[n], sems.at[n]) for n in range(CHUNKS * TILES)
    ]
    for copy in copies:
        copy.start()
    for copy in copies:
        copy.wait()


def make_blank(after):
    return pl.pallas_call(
        blank_kernel,
        out_shape=pltpu.HBM((CHUNKS * TILES, SIDE, SIDE), jnp.bfloat16),
        in_specs=[pl.BlockSpec(memory_space=pltpu.SMEM)],
        out_specs=pl.BlockSpec(memory_space=pltpu.HBM),
        scratch_shapes=[
            pltpu.VMEM((SIDE, SIDE), jnp.bfloat16),
            pltpu.SemaphoreType.DMA((CHUNKS * TILES,)),
        ],
        compiler_params=pltpu.CompilerParams(vmem_limit_bytes=16 * MIB),
    )(after)


def shards(
    templates,
    science,
    intersection,
    row_warp,
    col_warp,
    warps,
    taps,
    basis_row,
    basis_col,
    coef,
    home,
):
    me = lax.axis_index("det")
    where = jnp.stack([me // RING, me % RING]).astype(jnp.int32)

    with jax.named_scope("gather_templates"):
        tiles = (templates[0], templates[1])
        following = next_patch(templates)
        before = [along(tiles[0], "z", 1), None]
        after = [None, along(tiles[1], "z", -1)]
        before[1] = along(tiles[1], "z", 1)
        after[0] = along(tiles[0], "z", -1)
        far = [along(before[0], "z", 1), along(after[1], "z", -1)]
        here = (templates, *before, *after, *far)
        there = (following,) + tuple(next_patch(block) for block in here[1:])

    with jax.named_scope("spread_tables"):
        table = jnp.concatenate([intersection, row_warp, col_warp, home[:, None]], axis=1)
        table, _, _ = together(table, *far)
        meta = all_rows(table, "det")
        homes = meta[:, :, 3 * PER_TILE]
        target = homes[:, 0] // TILES
        side = homes % TILES
        same = (target[:, None] == target[None, :]).astype(jnp.int32)
        place_in = jnp.sum(jnp.tril(same, -1), axis=1)
        busiest = jnp.max(jnp.sum(same, axis=1)).reshape(1)

    with jax.named_scope("warp"):
        opposite = warp_partials((2,), where, meta, here + there, warps)
        nearer = warp_partials((0, 1, 3), where, meta, here + there, warps)

    with jax.named_scope("sum_partials"):
        busiest, _ = together(busiest, nearer[0])
        busiest = jnp.max(all_rows(busiest, "sky"))
        taps, seed, busiest = together(taps, where, busiest)
        bands = make_bands(taps)
        blank = make_blank(seed)
        up = along(opposite[0], "y", 1)
        down = along(opposite[1], "y", -1)

        def plus(a, b):
            return (a.astype(jnp.float32) + b.astype(jnp.float32)).astype(jnp.bfloat16)

        parts = (
            nearer[0],
            along(plus(nearer[2], up), "y", 1),
            along(nearer[4], "y", -1),
            nearer[1],
            along(nearer[3], "y", 1),
            along(plus(nearer[5], down), "y", -1),
        )

    with jax.named_scope("match"):
        pieces = match(where, basis_row, basis_col, coef, bands, parts, science)

    axes = ("y", "z")

    with jax.named_scope("spread_differences"):
        held = []
        for t, axis in enumerate(axes):
            own = pieces[t * RING : (t + 1) * RING]
            arrived = [own[0]] + [along(own[k], axis, k) for k in range(1, RING)]
            held.append(jnp.stack(arrived))
        held = list(together(*held))
        for t, axis in enumerate(axes[::-1]):
            held[t] = [held[t]] + [along(held[t], axis, j) for j in range(1, RING)]

    def send(blocks):
        return [
            block if n % RING == 0 else along(block, axes[n // RING], n % RING)
            for n, block in enumerate(blocks)
        ]

    with jax.named_scope("give_back"):
        most, more = compose((MOST, MORE), where, target, place_in, held[0] + held[1])
        most = send(most)
        more = lax.cond(busiest > MORE[0], send, list, list(more))
        returned = put((MOST, MORE), where, target, place_in, side, (most, more), blank)

    def rest(held, returned):
        (blocks,) = compose((REST,), where, target, place_in, held)
        return put((REST,), where, target, place_in, side, (send(blocks),), returned)

    with jax.named_scope("give_back_rest"):
        return lax.cond(
            busiest > REST[0], rest, lambda held, returned: returned, held[0] + held[1], returned
        )


def solution(mesh):
    placed = (
        P(("sky", "det"), None, None),
        P(("sky", "det"), None, None),
        P(("sky", "det"), None),
        P(("sky", "det"), None),
        P(("sky", "det"), None),
        P(),
        P(),
        P(("sky", "det"), None),
        P(("sky", "det"), None),
        P(("sky", "det"), None, None),
        P(("sky", "det")),
    )
    return jax.shard_map(
        shards, mesh=mesh, in_specs=placed, out_specs=P(("sky", "det"), None, None), check_vma=False
    )
```

```python
import functools
import itertools

import jax
import jax.numpy as jnp
from jax import lax
from jax.experimental import pallas as pl
from jax.experimental.pallas import tpu as pltpu
from jax.sharding import PartitionSpec as P

SIDE = 512
RING = 4
TILES = 2
PER_TILE = 4
BASES = 5
REACH = 10
CHUNKS = RING * RING
QUARTER = SIDE // RING
BANK = 8
MOST, MORE, REST = (0, 4), (4, 5), (5, CHUNKS)
DEEP = 4
MIB = 1024 * 1024


def place(z, y):
    return (z % RING) * RING + y % RING


def hop(block, dz, dy):
    route = [
        (place(z, y), place(z + dz, y + dy)) for z in range(RING) for y in range(RING)
    ]
    return lax.ppermute(block, "det", route)


def along(block, axis, step):
    return hop(block, step, 0) if axis == "z" else hop(block, 0, step)


def next_patch(block):
    count = lax.axis_size("sky")
    return lax.ppermute(block, "sky", [((i + 1) % count, i) for i in range(count)])


def all_rows(row, axis):
    copies = jnp.broadcast_to(row, (lax.axis_size(axis), *row.shape))
    return lax.all_to_all(copies, axis, split_axis=0, concat_axis=0, tiled=True)


def together(*arrays):
    return lax.optimization_barrier(arrays)


def bands_kernel(taps, out):
    shape = (SIDE, SIDE)
    rows = lax.broadcasted_iota(jnp.int32, shape, 0)
    cols = lax.broadcasted_iota(jnp.int32, shape, 1)
    rolled = pltpu.roll(jnp.broadcast_to(taps[0], shape), 0, 1, stride=1, stride_axis=0)
    out[...] = jnp.where(jnp.abs(cols - rows) <= REACH, rolled, 0.0).astype(jnp.bfloat16)


def make_bands(taps):
    filters, width = taps.shape
    assert width == 2 * REACH + 1
    first_rows = jnp.roll(jnp.pad(taps, ((0, 0), (0, SIDE - width))), -REACH, axis=1)
    return pl.pallas_call(
        bands_kernel,
        out_shape=jax.ShapeDtypeStruct((filters, SIDE, SIDE), jnp.bfloat16),
        grid=(filters,),
        in_specs=[pl.BlockSpec((1, 1, SIDE), lambda f: (f, 0, 0))],
        out_specs=pl.BlockSpec((None, SIDE, SIDE), lambda f: (f, 0, 0)),
        compiler_params=pltpu.CompilerParams(vmem_limit_bytes=16 * MIB),
    )(first_rows.reshape(filters, 1, SIDE))


def warp_kernel(steps, where, meta, *refs):
    rows = len(steps) * TILES
    cands, warps, outs, scratch = refs[:14], refs[14], refs[15 : 15 + rows], refs[15 + rows :]
    picks, ready, tile, bank, acc, sems, bank_sems = scratch
    z, y = where[0], where[1]
    count = jnp.int32(0)
    for n, step in enumerate(steps):
        for t in range(TILES):
            for k in range(PER_TILE):
                far_y = (y + step) % RING
                row = z * RING + far_y
                q = meta[row, t, k]
                owner = (q // TILES) % CHUNKS
                picks[0, count] = (
                    q // (TILES * CHUNKS) * (RING * TILES)
                    + ((owner // RING - z + RING) % RING) * TILES
                    + q % TILES
                )
                picks[1, count] = meta[row, t, PER_TILE + k]
                picks[2, count] = meta[row, t, 2 * PER_TILE + k]
                picks[3, count] = n * TILES + t
                count = count + (owner % RING == y).astype(jnp.int32)

    def bank_copy(n):
        return pltpu.make_async_copy(warps.at[n], bank.at[n], bank_sems.at[n])

    def need(n):
        @pl.when(ready[n] == 0)
        def _():
            bank_copy(n).wait()
            ready[n] = 1

    def copy(slot, source):
        return pltpu.make_async_copy(source, tile.at[slot], sems.at[slot])

    def start(i, slot):
        source = picks[0, i]
        for which in range(2):
            for dz, local in itertools.product(range(RING), range(TILES)):
                if dz == 0:
                    block = cands[7 * which].at[local]
                else:
                    block = cands[7 * which + {3: 1, 1: 3, 2: 5}[dz] + local]

                @pl.when(source == (which * RING + dz) * TILES + local)
                def _():
                    copy(slot, block).start()

    for i in range(DEEP - 1):

        @pl.when(i < count)
        def _():
            start(i, i)

    for n in range(BANK):
        bank_copy(n).start()
        ready[n] = 0

    acc[...] = jnp.zeros_like(acc)

    def body(i, carry):
        slot = lax.rem(i, DEEP)
        copy(slot, cands[0].at[0]).wait()

        @pl.when(i + DEEP - 1 < count)
        def _():
            start(i + DEEP - 1, lax.rem(i + DEEP - 1, DEEP))

        need(picks[1, i])
        need(picks[2, i])
        inner = jnp.dot(bank[picks[1, i]], tile[slot], preferred_element_type=jnp.float32)
        piece = lax.dot_general(
            inner.astype(jnp.bfloat16),
            bank[picks[2, i]],
            (((1,), (1,)), ((), ())),
            preferred_element_type=jnp.float32,
        )
        target = picks[3, i]
        acc[target] = acc[target] + piece
        return carry

    lax.fori_loop(0, count, body, 0)
    for n in range(BANK):
        need(n)
    for n, out in enumerate(outs):
        out[...] = acc[n].astype(jnp.bfloat16)


def warp_partials(steps, where, meta, cands, warps):
    rows = len(steps) * TILES
    scalars = pl.BlockSpec(memory_space=pltpu.SMEM)
    return pl.pallas_call(
        functools.partial(warp_kernel, steps),
        out_shape=[jax.ShapeDtypeStruct((SIDE, SIDE), jnp.bfloat16)] * rows,
        in_specs=[scalars, scalars]
        + [pl.BlockSpec(memory_space=pltpu.HBM)] * (len(cands) + 1),
        out_specs=[pl.BlockSpec(memory_space=pltpu.VMEM)] * rows,
        scratch_shapes=[
            pltpu.SMEM((4, rows * PER_TILE + 1), jnp.int32),
            pltpu.SMEM((BANK,), jnp.int32),
            pltpu.VMEM((DEEP, SIDE, SIDE), jnp.bfloat16),
            pltpu.VMEM((BANK, SIDE, SIDE), jnp.bfloat16),
            pltpu.VMEM((rows, SIDE, SIDE), jnp.float32),
            pltpu.SemaphoreType.DMA((DEEP,)),
            pltpu.SemaphoreType.DMA((BANK,)),
        ],
        compiler_params=pltpu.CompilerParams(vmem_limit_bytes=28 * MIB),
        cost_estimate=pl.CostEstimate(
            flops=rows * 4 * SIDE**3, bytes_accessed=rows * 4 * SIDE**2 * 2, transcendentals=0
        ),
    )(where, meta, *[pltpu.with_memory_space_constraint(x, pltpu.HBM) for x in (*cands, warps)])


def match_kernel(where, picks, coef, bands, *refs):
    parts, science, outs, (whole, model) = refs[:6], refs[6], refs[7:15], refs[15:]
    ui = (2.0 * lax.broadcasted_iota(jnp.int32, (SIDE, 1), 0).astype(jnp.float32) + 1.0) / SIDE - 1.0
    uj = (2.0 * lax.broadcasted_iota(jnp.int32, (1, SIDE), 1).astype(jnp.float32) + 1.0) / SIDE - 1.0
    for t in range(TILES):
        first, second, third = parts[3 * t : 3 * t + 3]
        total = first[...].astype(jnp.float32) + second[...].astype(jnp.float32)
        warped = (total + third[...].astype(jnp.float32)).astype(jnp.bfloat16)
        for b in range(BASES):
            half = jnp.dot(bands[picks[0, t, b]], warped, preferred_element_type=jnp.float32)
            conv = lax.dot_general(
                half.astype(jnp.bfloat16),
                bands[picks[1, t, b]],
                (((1,), (1,)), ((), ())),
                preferred_element_type=jnp.float32,
            )
            term = (coef[t, b, 0] + coef[t, b, 1] * ui + coef[t, b, 2] * uj) * conv
            if b == 0:
                model[...] = term
            elif b < BASES - 1:
                model[...] += term
            else:
                left = science[t].astype(jnp.float32) - (model[...] + term)
                whole[...] = left.astype(jnp.bfloat16)
        for k in range(RING):
            quarter = (where[1 - t] + k) % RING
            outs[t * RING + k][...] = whole[pl.ds(quarter * QUARTER, QUARTER)]


def match(where, rows, cols, coef, bands, parts, science):
    whole = pl.BlockSpec(memory_space=pltpu.VMEM)
    scalars = pl.BlockSpec(memory_space=pltpu.SMEM)
    return pl.pallas_call(
        match_kernel,
        out_shape=[jax.ShapeDtypeStruct((QUARTER, SIDE), jnp.bfloat16)] * (TILES * RING),
        in_specs=[scalars] * 3 + [whole] * 8,
        out_specs=[whole] * (TILES * RING),
        scratch_shapes=[
            pltpu.VMEM((SIDE, SIDE), jnp.bfloat16),
            pltpu.VMEM((SIDE, SIDE), jnp.float32),
        ],
        compiler_params=pltpu.CompilerParams(vmem_limit_bytes=28 * MIB),
        cost_estimate=pl.CostEstimate(
            flops=TILES * BASES * 4 * SIDE**3,
            bytes_accessed=(8 + 5) * SIDE**2 * 2,
            transcendentals=0,
        ),
    )(where, jnp.stack([rows, cols]), coef, bands, *parts, science)


def compose_kernel(spans, where, target, place_in, *refs):
    held, outs, sems = refs[:8], refs[8:-1], refs[-1]
    z, y = where[0], where[1]

    def each(t, j, action):
        for k in range(RING):
            source_z, source_y = (z - j, y - k) if t == 0 else (z - k, y - j)
            source = ((source_z + RING) % RING) * RING + (source_y + RING) % RING
            goal = target[source]
            if t == 0:
                live, step = goal // RING == z, (goal % RING - y + RING) % RING
            else:
                live, step = goal % RING == y, (goal // RING - z + RING) % RING
            slot = place_in[source]
            live = live & (slot >= spans[0][0]) & (slot < spans[-1][1])

            @pl.when(live)
            def _():
                action(t, j, k, step, slot)

    def copy(t, j, k, m, span, slot):
        goal = outs[(span * TILES + t) * RING + m].at[slot]
        n = (t * RING + j) * RING + k
        return pltpu.make_async_copy(held[t * RING + j].at[k], goal, sems.at[n])

    def begin(t, j, k, step, slot):
        for span, (low, high) in enumerate(spans):
            for m in range(RING):

                @pl.when((step == m) & (slot >= low) & (slot < high))
                def _():
                    copy(t, j, k, m, span, slot - low).start()

    def finish(t, j, k, step, slot):
        copy(t, j, k, 0, 0, 0).wait()

    for action in (begin, finish):
        for t, j in itertools.product(range(TILES), range(RING)):
            each(t, j, action)


def compose(spans, where, target, place_in, held):
    memory = pl.BlockSpec(memory_space=pltpu.VMEM)
    scalars = pl.BlockSpec(memory_space=pltpu.SMEM)
    shapes, specs = [], []
    for (low, high), _, m in itertools.product(spans, range(TILES), range(RING)):
        shape = (high - low, QUARTER, SIDE)
        stays = m == 0
        shapes.append(
            jax.ShapeDtypeStruct(shape, jnp.bfloat16) if stays else pltpu.HBM(shape, jnp.bfloat16)
        )
        specs.append(memory if stays else pl.BlockSpec(memory_space=pltpu.HBM))
    outs = pl.pallas_call(
        functools.partial(compose_kernel, spans),
        out_shape=shapes,
        in_specs=[scalars] * 3 + [memory] * len(held),
        out_specs=specs,
        scratch_shapes=[pltpu.SemaphoreType.DMA((TILES * CHUNKS,))],
        compiler_params=pltpu.CompilerParams(vmem_limit_bytes=16 * MIB),
    )(where, target, place_in, *held)
    width = TILES * RING
    return [outs[n * width : (n + 1) * width] for n in range(len(spans))]


def put_kernel(spans, where, target, place_in, side, *refs):
    arrived, (_, out, sems) = refs[:-3], refs[-3:]
    me = where[0] * RING + where[1]

    def copy(d, t, m, span, slot):
        quarter = (where[1 - t] - m + RING) % RING
        return pltpu.make_async_copy(
            arrived[(span * TILES + t) * RING + m].at[slot],
            out.at[d * TILES + side[d, t], pl.ds(quarter * QUARTER, QUARTER)],
            sems.at[d * TILES + t, m],
        )

    def begin(d):
        slot = place_in[d]
        for span, (low, high) in enumerate(spans):

            @pl.when((slot >= low) & (slot < high))
            def _():
                for t, m in itertools.product(range(TILES), range(RING)):
                    copy(d, t, m, span, slot - low).start()

    def finish(d):
        for t, m in itertools.product(range(TILES), range(RING)):
            copy(d, t, m, 0, 0).wait()

    for action in (begin, finish):

        for d in range(CHUNKS):
            slot = place_in[d]
            live = (target[d] == me) & (slot >= spans[0][0]) & (slot < spans[-1][1])

            @pl.when(live)
            def _():
                action(d)


def put(spans, where, target, place_in, side, arrived, blank):
    scalars = pl.BlockSpec(memory_space=pltpu.SMEM)
    arrays = [block for span in arrived for block in span]
    return pl.pallas_call(
        functools.partial(put_kernel, spans),
        out_shape=pltpu.HBM(blank.shape, blank.dtype),
        in_specs=[scalars] * 4
        + [pl.BlockSpec(memory_space=pltpu.VMEM)] * len(arrays)
        + [pl.BlockSpec(memory_space=pltpu.HBM)],
        out_specs=pl.BlockSpec(memory_space=pltpu.HBM),
        scratch_shapes=[pltpu.SemaphoreType.DMA((CHUNKS * TILES, RING))],
        input_output_aliases={4 + len(arrays): 0},
        compiler_params=pltpu.CompilerParams(vmem_limit_bytes=24 * MIB),
    )(where, target, place_in, side, *arrays, blank)


def blank_kernel(_, out, zeros, sems):
    zeros[...] = jnp.zeros_like(zeros)
    copies = [
        pltpu.make_async_copy(zeros, out.at[n], sems.at[n]) for n in range(CHUNKS * TILES)
    ]
    for copy in copies:
        copy.start()
    for copy in copies:
        copy.wait()


def make_blank(after):
    return pl.pallas_call(
        blank_kernel,
        out_shape=pltpu.HBM((CHUNKS * TILES, SIDE, SIDE), jnp.bfloat16),
        in_specs=[pl.BlockSpec(memory_space=pltpu.SMEM)],
        out_specs=pl.BlockSpec(memory_space=pltpu.HBM),
        scratch_shapes=[
            pltpu.VMEM((SIDE, SIDE), jnp.bfloat16),
            pltpu.SemaphoreType.DMA((CHUNKS * TILES,)),
        ],
        compiler_params=pltpu.CompilerParams(vmem_limit_bytes=16 * MIB),
    )(after)


def shards(
    templates,
    science,
    intersection,
    row_warp,
    col_warp,
    warps,
    taps,
    basis_row,
    basis_col,
    coef,
    home,
):
    me = lax.axis_index("det")
    where = jnp.stack([me // RING, me % RING]).astype(jnp.int32)

    with jax.named_scope("gather_templates"):
        tiles = (templates[0], templates[1])
        following = next_patch(templates)
        before = [None, along(tiles[1], "z", 1)]
        after = [along(tiles[0], "z", -1), None]
        before[0] = along(tiles[0], "z", 1)
        after[1] = along(tiles[1], "z", -1)
        far = [along(before[0], "z", 1), along(after[1], "z", -1)]
        here = (templates, *before, *after, *far)
        there = (following,) + tuple(next_patch(block) for block in here[1:])

    with jax.named_scope("spread_tables"):
        table = jnp.concatenate([intersection, row_warp, col_warp, home[:, None]], axis=1)
        table, _, _ = together(table, before[0], after[1])
        meta = all_rows(table, "det")
        homes = meta[:, :, 3 * PER_TILE]
        target = homes[:, 0] // TILES
        side = homes % TILES
        same = (target[:, None] == target[None, :]).astype(jnp.int32)
        place_in = jnp.sum(jnp.tril(same, -1), axis=1)
        busiest = jnp.max(jnp.sum(same, axis=1)).reshape(1)

    with jax.named_scope("warp"):
        opposite = warp_partials((2,), where, meta, here + there, warps)
        nearer = warp_partials((0, 1, 3), where, meta, here + there, warps)

    with jax.named_scope("sum_partials"):
        busiest, _ = together(busiest, nearer[0])
        busiest = jnp.max(all_rows(busiest, "sky"))
        taps, busiest = together(taps, busiest)
        bands = make_bands(taps)
        up = along(opposite[0], "y", 1)
        down = along(opposite[1], "y", -1)

        def plus(a, b):
            return (a.astype(jnp.float32) + b.astype(jnp.float32)).astype(jnp.bfloat16)

        parts = (
            nearer[0],
            along(plus(nearer[2], up), "y", 1),
            along(nearer[4], "y", -1),
            nearer[1],
            along(nearer[3], "y", 1),
            along(plus(nearer[5], down), "y", -1),
        )

    with jax.named_scope("match"):
        pieces = match(where, basis_row, basis_col, coef, bands, parts, science)

    axes = ("y", "z")

    with jax.named_scope("spread_differences"):
        held = []
        for t, axis in enumerate(axes):
            own = pieces[t * RING : (t + 1) * RING]
            arrived = [own[0]] + [along(own[k], axis, k) for k in range(1, RING)]
            held.append(jnp.stack(arrived))
        *held, seed = together(*held, where)
        blank = make_blank(seed)
        for t, axis in enumerate(axes[::-1]):
            held[t] = [held[t]] + [along(held[t], axis, j) for j in range(1, RING)]

    def send(blocks):
        return [
            block if n % RING == 0 else along(block, axes[n // RING], n % RING)
            for n, block in enumerate(blocks)
        ]

    with jax.named_scope("give_back"):
        target, blank = together(target, blank)
        most, more = compose((MOST, MORE), where, target, place_in, held[0] + held[1])
        most = send(most)
        more = lax.cond(busiest > MORE[0], send, list, list(more))
        returned = put((MOST, MORE), where, target, place_in, side, (most, more), blank)

    def rest(held, returned):
        (blocks,) = compose((REST,), where, target, place_in, held)
        return put((REST,), where, target, place_in, side, (send(blocks),), returned)

    with jax.named_scope("give_back_rest"):
        return lax.cond(
            busiest > REST[0], rest, lambda held, returned: returned, held[0] + held[1], returned
        )


def solution(mesh):
    placed = (
        P(("sky", "det"), None, None),
        P(("sky", "det"), None, None),
        P(("sky", "det"), None),
        P(("sky", "det"), None),
        P(("sky", "det"), None),
        P(),
        P(),
        P(("sky", "det"), None),
        P(("sky", "det"), None),
        P(("sky", "det"), None, None),
        P(("sky", "det")),
    )
    return jax.shard_map(
        shards, mesh=mesh, in_specs=placed, out_specs=P(("sky", "det"), None, None), check_vma=False
    )
```
